32 devices in a mesh: tx: 8 (over y, x, core), ty: 4 (over z).
Axes of the slice: x: 2, y: 2, z: 4, core: 2. Of those that a mesh axis runs over, the one named last changes fastest.
Arguments:
- volume: bfloat16 [256, 128, 16, 64], P('tx', 'ty'), may hold values from -6 to 6
- first_weight: bfloat16 [2, 2, 2, 64, 128], replicated, may hold values from -0.375 to 0.375
- first_bias: float32 [128], replicated, may hold values from -1.5 to 1.5
- second_weight: bfloat16 [2, 2, 2, 128, 256], replicated, may hold values from -0.25 to 0.25
- second_bias: float32 [256], replicated, may hold values from -1.5 to 1.5
- inner_weight: bfloat16 [3, 3, 3, 256, 256], replicated, may hold values from -0.109375 to 0.109375
- inner_bias: float32 [256], replicated, may hold values from -1.5 to 1.5
- outer_weight: bfloat16 [3, 3, 3, 256, 256], replicated, may hold values from -0.109375 to 0.109375
- outer_bias: float32 [256], replicated, may hold values from -1.5 to 1.5
Outputs:
- encoded: bfloat16 [64, 32, 4, 256], P('tx', 'ty')
The draws below stay inside these ranges and needn't reach their ends.
All inputs are finite; a program needn't handle non-finite values.
Results may differ from the reference program's by a relative error of at most 0.0058.
Values may be sent and summed in bfloat16 or wider, within the bound.
A program may use at most 64 MiB of HBM per device.

```python
import jax
import jax.numpy as jnp
from jax import lax

CIN = 64
C1 = 128
C2 = 256
DILATION_RATE = 2
FZ = 16
NX = 256
NY = 128
KX = 64
KY = 32
KZ = 4


def level_of(own_key, extent, cuts, low, top_value):
    def one(dim, shards_of):
        draws = jax.random.uniform(jax.random.fold_in(jax.random.fold_in(own_key, 6), dim), (shards_of,), jnp.float32, low / len(cuts), top_value / len(cuts))
        return jnp.repeat(jnp.exp(draws), extent[dim] // shards_of).reshape((-1,) + (1,) * (len(extent) - dim - 1))

    loudness = one(*cuts[0])
    for cut in cuts[1:]:
        loudness = loudness * one(*cut)
    return loudness


def scatter_about(key, shape, scale, bound, cuts=(), dtype=jnp.bfloat16):
    values = jax.random.normal(key, shape, jnp.float32) * scale
    if len(cuts) > 0:
        values = level_of(key, shape, cuts, -0.22, 0.18) * values
    return jnp.clip(values, min=-bound, max=bound).astype(dtype)


def setup_inputs(seed: int = 0) -> dict:
    seeds = jax.random.split(jax.random.key(seed), 10)
    return {
        "volume": scatter_about(seeds[0], (NX, NY, FZ, CIN), 1.0, 6.0, ((0, 8), (1, 4))),
        "first_weight": scatter_about(seeds[1], (2, 2, 2, CIN, C1), (4 * CIN) ** -0.5, 0.375),
        "first_bias": scatter_about(seeds[2], (C1,), 0.3, 1.5, (), jnp.float32),
        "second_weight": scatter_about(seeds[3], (2, 2, 2, C1, C2), (4 * C1) ** -0.5, 0.25),
        "second_bias": scatter_about(seeds[4], (C2,), 0.3, 1.5, (), jnp.float32),
        "inner_weight": scatter_about(seeds[5], (3, 3, 3, C2, C2), (27 * C2 // 2) ** -0.5, 0.109375),
        "inner_bias": scatter_about(seeds[6], (C2,), 0.3, 1.5, (), jnp.float32),
        "outer_weight": scatter_about(seeds[7], (3, 3, 3, C2, C2), (27 * C2 // 2) ** -0.5, 0.109375),
        "outer_bias": scatter_about(seeds[8], (C2,), 0.3, 1.5, (), jnp.float32),
    }


def leaky(values):
    return jnp.where(values > 0, values, 0.01 * values)


def strided(feature_field, weight, bias):
    size_x, size_y, size_z, chans = feature_field.shape
    blocks = feature_field.reshape(size_x // 2, 2, size_y // 2, 2, size_z // 2, 2, chans)
    blocks = blocks.transpose(0, 2, 4, 1, 3, 5, 6).reshape(-1, 8 * chans)
    total = jnp.dot(blocks, weight.reshape(8 * chans, -1), preferred_element_type=jnp.float32)
    return leaky(total + bias).astype(jnp.bfloat16).reshape(size_x // 2, size_y // 2, size_z // 2, -1)


def dilated_sum(padded_volume, weight):
    output_x = padded_volume.shape[0] - 2 * DILATION_RATE
    output_y = padded_volume.shape[1] - 2 * DILATION_RATE
    output_z = padded_volume.shape[2] - 2 * DILATION_RATE
    chans = padded_volume.shape[3]
    total = jnp.zeros((output_x * output_y * output_z, weight.shape[4]), jnp.float32)
    for shift_along_x in range(3):
        for shift_along_y in range(3):
            for shift_along_z in range(3):
                volume_portion = padded_volume[shift_along_x * DILATION_RATE:shift_along_x * DILATION_RATE + output_x, shift_along_y * DILATION_RATE:shift_along_y * DILATION_RATE + output_y, shift_along_z * DILATION_RATE:shift_along_z * DILATION_RATE + output_z, :]
                total = total + jnp.dot(volume_portion.reshape(-1, chans), weight[shift_along_x, shift_along_y, shift_along_z], preferred_element_type=jnp.float32)
    return total.reshape(output_x, output_y, output_z, -1)


def pad_all(feature_field):
    return jnp.pad(feature_field, ((DILATION_RATE, DILATION_RATE), (DILATION_RATE, DILATION_RATE), (DILATION_RATE, DILATION_RATE), (0, 0)))


def reference(volume, first_weight, first_bias, second_weight, second_bias, inner_weight, inner_bias, outer_weight, outer_bias):
    def section(slab):
        return strided(strided(slab, first_weight, first_bias), second_weight, second_bias)

    coarse_volume = lax.map(section, volume.reshape(NX // 32, 32, NY, FZ, CIN)).reshape(KX, KY, KZ, C2)
    hidden_activation = leaky(dilated_sum(pad_all(coarse_volume), inner_weight) + inner_bias).astype(jnp.bfloat16)
    result = leaky(coarse_volume.astype(jnp.float32) + dilated_sum(pad_all(hidden_activation), outer_weight) + outer_bias)
    return result.astype(jnp.bfloat16)
```

```python
import jax
import jax.numpy as jnp
from jax import lax
from jax.experimental import pallas as pl
from jax.experimental.pallas import tpu as pltpu
from jax.sharding import PartitionSpec as P

DIRECTIONS = ((-1, 0), (1, 0), (0, -1), (0, 1), (-1, -1), (-1, 1), (1, -1), (1, 1))
OPPOSITE = (1, 0, 3, 2, 7, 6, 5, 4)
BF = jnp.bfloat16
F32 = jnp.float32


def leaky(values):
    return jnp.where(values > 0, values, 0.01 * values)


def kernel(
    volume, w1, b1, w2, b2, wi, bi, wo, bo,
    out,
    vbuf, w1b, w2b, wib, wob, b1b, b2b, bib, bob,
    sums, blocks, pads, edge_out, edge_in, corner_out, corner_in,
    load_sem, send_sem, recv_sem,
):
    ix, iy = lax.axis_index("tx"), lax.axis_index("ty")
    nx, ny = lax.axis_size("tx"), lax.axis_size("ty")
    groups_x, groups_y = pads.shape[2] - 2, pads.shape[3] - 2
    half = groups_x * groups_y * 8

    def exists(d):
        dx, dy = DIRECTIONS[d]
        test = None
        for delta, i, n in ((dx, ix, nx), (dy, iy, ny)):
            if delta:
                one = i >= 1 if delta < 0 else i <= n - 2
                test = one if test is None else jnp.logical_and(test, one)
        return test

    def device(d):
        return {"tx": ix + DIRECTIONS[d][0], "ty": iy + DIRECTIONS[d][1]}

    loads = []

    def load(src, dst):
        copy = pltpu.make_async_copy(src, dst, load_sem.at[len(loads)])
        copy.start()
        loads.append(copy)
        return copy

    load_w1, load_b1 = load(w1, w1b), load(b1, b1b)
    load_v = [load(volume.at[pl.ds(8 * i, 8)], vbuf.at[i]) for i in range(groups_x)]
    load_w2, load_b2 = load(w2, w2b), load(b2, b2b)
    load_bi, load_bo = load(bi, bib), load(bo, bob)
    load_wi = {a: load(wi.at[a], wib.at[a]) for a in (1, 0, 2)}
    load_wo = {a: load(wo.at[a], wob.at[a]) for a in (1, 0, 2)}

    barrier = pltpu.get_barrier_semaphore()
    count = 0
    for d in range(8):
        count = count + exists(d).astype(jnp.int32)

        @pl.when(exists(d))
        def _():
            pl.semaphore_signal(
                barrier, inc=1, device_id=device(d), device_id_type=pl.DeviceIdType.MESH
            )

    pads[...] = jnp.zeros_like(pads)

    load_w1.wait()
    load_b1.wait()
    w1cat = jnp.concatenate(
        [
            jnp.concatenate([w1b[p, q, 0], w1b[p, q, 1]], axis=1)
            for p in range(2)
            for q in range(2)
        ],
        axis=0,
    )
    rows_y = 2 * groups_y
    bias1 = b1b[...]
    for i in range(groups_x):
        load_v[i].wait()
        for xp in range(2):
            slabs = [
                vbuf[i, 4 * xp + j].reshape(rows_y, 4, 16, 64) for j in range(4)
            ]
            for pc in range(2):
                for qc in range(2):
                    lhs = jnp.concatenate(
                        [
                            slabs[2 * pc + p][:, 2 * qc + q].reshape(rows_y * 16, 64)
                            for p in range(2)
                            for q in range(2)
                        ],
                        axis=1,
                    )
                    slot = (i * 2 + xp) * 4 + pc * 2 + qc
                    both = jnp.dot(lhs, w1cat, preferred_element_type=F32)
                    sums[slot, 0] = both[:, 0:128]
                    sums[slot, 1] = both[:, 128:256]
            for pc in range(2):
                for qc in range(2):
                    slot = (i * 2 + xp) * 4 + pc * 2 + qc
                    for rc in range(2):
                        even = sums[slot, 0, pl.ds(2 * rc, 4 * rows_y, stride=4)]
                        odd = sums[slot, 1, pl.ds(2 * rc + 1, 4 * rows_y, stride=4)]
                        finer = leaky(even + odd + bias1).astype(BF)
                        k = (pc * 2 + qc) * 2 + rc
                        row = (i * 2 + xp) * 4 * rows_y
                        blocks[row : row + 4 * rows_y, k * 128 : k * 128 + 128] = finer

    load_w2.wait()
    load_b2.wait()
    total = jnp.dot(
        blocks[...], w2b[...].reshape(8 * 128, 256), preferred_element_type=F32
    )
    coarse = leaky(total + b2b[...]).astype(BF).astype(F32)
    coarse = coarse.reshape(groups_x, 2, groups_y * 8, 256)
    even_x = coarse[:, 0].reshape(half, 256)
    odd_x = coarse[:, 1].reshape(half, 256)
    keep = (lax.broadcasted_iota(jnp.int32, (half, 256), 0) // 2) % 2 == 0
    cells = (
        jnp.where(keep, even_x, pltpu.roll(odd_x, 2, 0)),
        jnp.where(keep, pltpu.roll(even_x, half - 2, 0), odd_x),
    )

    def copy_of(e, d, incoming):
        slot = d if incoming else OPPOSITE[d]
        if d < 4:
            src, dst = edge_out.at[e, d], edge_in.at[e, slot]
        else:
            src, dst = corner_out.at[e, d - 4], corner_in.at[e, slot - 4]
        return pltpu.make_async_remote_copy(
            src_ref=src,
            dst_ref=dst,
            send_sem=send_sem.at[e, d],
            recv_sem=recv_sem.at[e, slot],
            device_id=device(d),
            device_id_type=pl.DeviceIdType.MESH,
        )

    def publish(e, cells):
        parts = [c.reshape(groups_x, groups_y, 8, 256) for c in cells]
        for d in (4, 5, 6, 7, 2, 3, 0, 1):
            dx, dy = DIRECTIONS[d]
            sx = slice(0, 1) if dx < 0 else slice(groups_x - 1, groups_x) if dx else slice(None)
            sy = slice(0, 1) if dy < 0 else slice(groups_y - 1, groups_y) if dy else slice(None)
            block = jnp.concatenate(
                [part[sx, sy].reshape(-1, 256) for part in parts], axis=0
            ).astype(BF)
            if d < 4:
                edge_out[e, d] = block
            else:
                corner_out[e, d - 4] = block

            @pl.when(exists(d))
            def _():
                copy_of(e, d, False).start()

        for z in range(2):
            pads[e, z, 1 : 1 + groups_x, 1 : 1 + groups_y] = parts[z]

    def receive(e, d):
        dx, dy = DIRECTIONS[d]
        px = slice(0, 1) if dx < 0 else slice(groups_x + 1, groups_x + 2) if dx else slice(1, 1 + groups_x)
        py = slice(0, 1) if dy < 0 else slice(groups_y + 1, groups_y + 2) if dy else slice(1, 1 + groups_y)

        @pl.when(exists(d))
        def _():
            copy_of(e, d, True).wait_recv()
            block = (edge_in[e, d] if d < 4 else corner_in[e, d - 4]).astype(F32)
            rows = block.shape[0] // 2
            for z in range(2):
                shape = (px.stop - px.start, py.stop - py.start, 8, 256)
                pads[e, z, px, py] = block[z * rows : z * rows + rows].reshape(shape)

    def taps(e, weight, which, totals):
        for a, b in which:
            lhs = jnp.concatenate(
                [
                    pads[e, z, a : a + groups_x, b : b + groups_y].reshape(half, 256).astype(BF)
                    for z in range(2)
                ],
                axis=1,
            )
            lower = weight[a, b, 1:3].reshape(512, 256)
            upper = weight[a, b, 0:2].reshape(512, 256)
            totals = (
                totals[0] + jnp.dot(lhs, lower, preferred_element_type=F32),
                totals[1] + jnp.dot(lhs, upper, preferred_element_type=F32),
            )
        return totals

    def dilated(e, weight, arrivals, start):
        arrivals[1].wait()
        totals = taps(e, weight, ((1, 1),), start)
        for d in (0, 1, 2, 3):
            receive(e, d)
        arrivals[0].wait()
        arrivals[2].wait()
        totals = taps(e, weight, ((0, 1), (2, 1), (1, 0), (1, 2)), totals)
        for d in (4, 5, 6, 7):
            receive(e, d)
        return taps(e, weight, ((0, 0), (0, 2), (2, 0), (2, 2)), totals)

    pl.semaphore_wait(barrier, count)
    publish(0, cells)
    load_bi.wait()
    load_bo.wait()
    inner = jnp.broadcast_to(bib[...], (half, 256))
    totals = dilated(0, wib, load_wi, (inner, inner))
    publish(1, [leaky(t).astype(BF).astype(F32) for t in totals])
    start = [
        pads[0, z, 1 : 1 + groups_x, 1 : 1 + groups_y].reshape(half, 256) + bob[...]
        for z in range(2)
    ]
    totals = dilated(1, wob, load_wo, start)
    lower, upper = leaky(totals[0]), leaky(totals[1])
    even_x = jnp.where(keep, lower, pltpu.roll(upper, 2, 0)).astype(BF)
    odd_x = jnp.where(keep, pltpu.roll(lower, half - 2, 0), upper).astype(BF)
    rows = groups_y * 8
    for i in range(groups_x):
        out[(2 * i) * rows : (2 * i + 1) * rows] = even_x[i * rows : (i + 1) * rows]
        out[(2 * i + 1) * rows : (2 * i + 2) * rows] = odd_x[i * rows : (i + 1) * rows]

    for e in range(2):
        for d in range(8):

            @pl.when(exists(d))
            def _():
                copy_of(e, d, False).wait_send()


def local(
    volume,
    first_weight,
    first_bias,
    second_weight,
    second_bias,
    inner_weight,
    inner_bias,
    outer_weight,
    outer_bias,
):
    size_x, size_y, size_z, chans = volume.shape
    gx, gy = size_x // 8, size_y // 8
    cells = gx * gy * 16
    any_spec = pl.BlockSpec(memory_space=pl.ANY)
    vmem = pltpu.VMEM
    result = pl.pallas_call(
        kernel,
        out_shape=jax.ShapeDtypeStruct((cells, 256), BF),
        in_specs=[any_spec] * 9,
        out_specs=pl.BlockSpec(memory_space=pltpu.VMEM),
        scratch_shapes=[
            vmem((gx, 8, size_y, size_z, chans), BF),
            vmem(first_weight.shape, BF),
            vmem(second_weight.shape, BF),
            vmem(inner_weight.shape, BF),
            vmem(outer_weight.shape, BF),
            vmem((1, 128), F32),
            vmem((1, 256), F32),
            vmem((1, 256), F32),
            vmem((1, 256), F32),
            vmem((gx * 8, 2, gy * 32, 128), F32),
            vmem((cells, 1024), BF),
            vmem((2, 2, gx + 2, gy + 2, 8, 256), F32),
            vmem((2, 4, gy * 16, 256), BF),
            vmem((2, 4, gy * 16, 256), BF),
            vmem((2, 4, 16, 256), BF),
            vmem((2, 4, 16, 256), BF),
            pltpu.SemaphoreType.DMA((gx + 12,)),
            pltpu.SemaphoreType.DMA((2, 8)),
            pltpu.SemaphoreType.DMA((2, 8)),
        ],
        compiler_params=pltpu.CompilerParams(
            collective_id=0, has_side_effects=True, vmem_limit_bytes=56 * 2**20
        ),
        cost_estimate=pl.CostEstimate(
            flops=2_000_000_000, bytes_accessed=12_000_000, transcendentals=0
        ),
    )(
        volume,
        first_weight,
        first_bias.reshape(1, -1),
        second_weight,
        second_bias.reshape(1, -1),
        inner_weight,
        inner_bias.reshape(1, -1),
        outer_weight,
        outer_bias.reshape(1, -1),
    )
    return result.reshape(size_x // 4, size_y // 4, size_z // 4, 256)


def solution(mesh):
    in_specs = (P("tx", "ty", None, None), P(), P(), P(), P(), P(), P(), P(), P())
    out_specs = P("tx", "ty", None, None)
    return jax.shard_map(local, mesh=mesh, in_specs=in_specs, out_specs=out_specs, check_vma=False)
```

```python
import jax
import jax.numpy as jnp
from jax import lax
from jax.experimental import pallas as pl
from jax.experimental.pallas import tpu as pltpu
from jax.sharding import PartitionSpec as P

DIRECTIONS = ((-1, 0), (1, 0), (0, -1), (0, 1), (-1, -1), (-1, 1), (1, -1), (1, 1))
ORDER = (4, 5, 6, 7, 2, 3, 0, 1)
OPPOSITE = (1, 0, 3, 2, 7, 6, 5, 4)
BF = jnp.bfloat16
F32 = jnp.float32


def leaky(values):
    return jnp.where(values > 0, values, 0.01 * values)


def kernel(
    volume, w1, b1, w2, b2, wi, bi, wo, bo,
    out,
    vbuf, w1b, w2b, wib, wob, b1b, b2b, bib, bob,
    sums, blocks, halo, inner, edge_out, edge_in, corner_out, corner_in,
    load_sem, send_sem, recv_sem,
):
    ix, iy = lax.axis_index("tx"), lax.axis_index("ty")
    nx, ny = lax.axis_size("tx"), lax.axis_size("ty")
    groups_x, groups_y = halo.shape[1] - 4, halo.shape[2] - 4
    half = groups_x * groups_y * 8

    def exists(d):
        dx, dy = DIRECTIONS[d]
        test = None
        for delta, i, n in ((dx, ix, nx), (dy, iy, ny)):
            if delta:
                one = i >= 1 if delta < 0 else i <= n - 2
                test = one if test is None else jnp.logical_and(test, one)
        return test

    def device(d):
        return {"tx": ix + DIRECTIONS[d][0], "ty": iy + DIRECTIONS[d][1]}

    loads = []

    def load(src, dst):
        copy = pltpu.make_async_copy(src, dst, load_sem.at[len(loads)])
        copy.start()
        loads.append(copy)
        return copy

    load_w1, load_b1 = load(w1, w1b), load(b1, b1b)
    load_v = [load(volume.at[pl.ds(8 * i, 8)], vbuf.at[i]) for i in range(groups_x)]
    load_w2, load_b2 = load(w2, w2b), load(b2, b2b)
    load_bi, load_bo = load(bi, bib), load(bo, bob)
    load_wi = {a: load(wi.at[a], wib.at[a]) for a in (1, 0, 2)}
    load_wo = {a: load(wo.at[a], wob.at[a]) for a in (1, 0, 2)}

    barrier = pltpu.get_barrier_semaphore()
    count = 0
    for d in range(8):
        count = count + exists(d).astype(jnp.int32)

        @pl.when(exists(d))
        def _():
            pl.semaphore_signal(
                barrier, inc=1, device_id=device(d), device_id_type=pl.DeviceIdType.MESH
            )

    halo[...] = jnp.zeros_like(halo)

    load_w1.wait()
    load_b1.wait()
    w1cat = jnp.concatenate(
        [
            jnp.concatenate([w1b[p, q, 0], w1b[p, q, 1]], axis=1)
            for p in range(2)
            for q in range(2)
        ],
        axis=0,
    )
    rows_y = 2 * groups_y
    bias1 = b1b[...]
    for i in range(groups_x):
        load_v[i].wait()
        for xp in range(2):
            slabs = [
                vbuf[i, 4 * xp + j].reshape(rows_y, 4, 16, 64) for j in range(4)
            ]
            for pc in range(2):
                for qc in range(2):
                    lhs = jnp.concatenate(
                        [
                            slabs[2 * pc + p][:, 2 * qc + q].reshape(rows_y * 16, 64)
                            for p in range(2)
                            for q in range(2)
                        ],
                        axis=1,
                    )
                    slot = (i * 2 + xp) * 4 + pc * 2 + qc
                    both = jnp.dot(lhs, w1cat, preferred_element_type=F32)
                    sums[slot, 0] = both[:, 0:128]
                    sums[slot, 1] = both[:, 128:256]
            for pc in range(2):
                for qc in range(2):
                    slot = (i * 2 + xp) * 4 + pc * 2 + qc
                    for rc in range(2):
                        even = sums[slot, 0, pl.ds(2 * rc, 4 * rows_y, stride=4)]
                        odd = sums[slot, 1, pl.ds(2 * rc + 1, 4 * rows_y, stride=4)]
                        finer = leaky(even + odd + bias1).astype(BF)
                        k = (pc * 2 + qc) * 2 + rc
                        row = (i * 2 + xp) * 4 * rows_y
                        blocks[row : row + 4 * rows_y, k * 128 : k * 128 + 128] = finer

    load_w2.wait()
    load_b2.wait()
    total = jnp.dot(
        blocks[...], w2b[...].reshape(8 * 128, 256), preferred_element_type=F32
    )
    coarse = leaky(total + b2b[...]).astype(BF).astype(F32)
    coarse = coarse.reshape(groups_x, 2, groups_y * 8, 256)
    even_x = coarse[:, 0].reshape(half, 256)
    odd_x = coarse[:, 1].reshape(half, 256)
    keep = (lax.broadcasted_iota(jnp.int32, (half, 256), 0) // 2) % 2 == 0
    cells = (
        jnp.where(keep, even_x, pltpu.roll(odd_x, 2, 0)),
        jnp.where(keep, pltpu.roll(even_x, half - 2, 0), odd_x),
    )

    def copy_of(d, incoming):
        slot = d if incoming else OPPOSITE[d]
        if d < 4:
            src, dst = edge_out.at[d], edge_in.at[slot]
        else:
            src, dst = corner_out.at[d - 4], corner_in.at[slot - 4]
        return pltpu.make_async_remote_copy(
            src_ref=src,
            dst_ref=dst,
            send_sem=send_sem.at[d],
            recv_sem=recv_sem.at[slot],
            device_id=device(d),
            device_id_type=pl.DeviceIdType.MESH,
        )

    def sent(delta, groups):
        return slice(0, 2) if delta < 0 else slice(groups - 2, groups) if delta else slice(0, groups)

    def landed(delta, groups):
        if delta < 0:
            return slice(0, 2)
        return slice(groups + 2, groups + 4) if delta else slice(2, 2 + groups)

    parts = [c.reshape(groups_x, groups_y, 8, 256) for c in cells]
    pl.semaphore_wait(barrier, count)
    for d in ORDER:
        dx, dy = DIRECTIONS[d]
        block = jnp.concatenate(
            [part[sent(dx, groups_x), sent(dy, groups_y)].reshape(-1, 256) for part in parts],
            axis=0,
        ).astype(BF)
        if d < 4:
            edge_out[d] = block
        else:
            corner_out[d - 4] = block

        @pl.when(exists(d))
        def _():
            copy_of(d, False).start()

    own = jnp.concatenate([c.astype(BF) for c in cells], axis=1)
    for z in range(2):
        halo[z, 2 : 2 + groups_x, 2 : 2 + groups_y] = parts[z]
    load_bi.wait()
    load_bo.wait()
    inner[...] = jnp.broadcast_to(bib[...].reshape(1, 1, 1, 1, 256), inner.shape)

    def both(lhs, weight, a, b):
        lower = weight[a, b, 1:3].reshape(512, 256)
        upper = weight[a, b, 0:2].reshape(512, 256)
        return (
            jnp.dot(lhs, lower, preferred_element_type=F32),
            jnp.dot(lhs, upper, preferred_element_type=F32),
        )

    for a in (1, 0, 2):
        load_wi[a].wait()
        for b in (1, 0, 2):
            for z, term in enumerate(both(own, wib, a, b)):
                inner[z, 2 - a : 2 - a + groups_x, 2 - b : 2 - b + groups_y] += term.reshape(
                    groups_x, groups_y, 8, 256
                )

    for d in ORDER:
        dx, dy = DIRECTIONS[d]
        px, py = landed(dx, groups_x), landed(dy, groups_y)

        @pl.when(exists(d))
        def _():
            copy_of(d, True).wait_recv()
            block = (edge_in[d] if d < 4 else corner_in[d - 4]).astype(F32)
            rows = block.shape[0] // 2
            for z in range(2):
                shape = (px.stop - px.start, py.stop - py.start, 8, 256)
                halo[z, px, py] = block[z * rows : z * rows + rows].reshape(shape)

    def outside(shift, groups):
        return [i for i in range(shift, shift + groups + 2) if not 2 <= i < 2 + groups]

    for a in (1, 0, 2):
        for b in (1, 0, 2):
            pieces = [
                (slice(i, i + 1), slice(b, b + groups_y + 2)) for i in outside(a, groups_x)
            ] + [
                (slice(2, 2 + groups_x), slice(i, i + 1)) for i in outside(b, groups_y)
            ]
            lhs = jnp.concatenate(
                [
                    jnp.concatenate(
                        [halo[z, sx, sy].reshape(-1, 256) for sx, sy in pieces], axis=0
                    ).astype(BF)
                    for z in range(2)
                ],
                axis=1,
            )
            for z, term in enumerate(both(lhs, wib, a, b)):
                row = 0
                for sx, sy in pieces:
                    shape = (sx.stop - sx.start, sy.stop - sy.start, 8, 256)
                    rows = shape[0] * shape[1] * 8
                    inner[
                        z, sx.start - a : sx.stop - a, sy.start - b : sy.stop - b
                    ] += term[row : row + rows].reshape(shape)
                    row += rows

    inner[...] = leaky(inner[...]).astype(BF).astype(F32)

    @pl.when(ix == 0)
    def _():
        inner[:, 0] = jnp.zeros_like(inner[:, 0])

    @pl.when(ix == nx - 1)
    def _():
        inner[:, groups_x + 1] = jnp.zeros_like(inner[:, 0])

    @pl.when(iy == 0)
    def _():
        inner[:, :, 0] = jnp.zeros_like(inner[:, :, 0])

    @pl.when(iy == ny - 1)
    def _():
        inner[:, :, groups_y + 1] = jnp.zeros_like(inner[:, :, 0])

    totals = [
        halo[z, 2 : 2 + groups_x, 2 : 2 + groups_y].reshape(half, 256) + bob[...]
        for z in range(2)
    ]
    for a in (1, 0, 2):
        load_wo[a].wait()
        for b in (1, 0, 2):
            lhs = jnp.concatenate(
                [
                    inner[z, a : a + groups_x, b : b + groups_y].reshape(half, 256).astype(BF)
                    for z in range(2)
                ],
                axis=1,
            )
            totals = [t + term for t, term in zip(totals, both(lhs, wob, a, b))]
    lower, upper = leaky(totals[0]), leaky(totals[1])
    even_x = jnp.where(keep, lower, pltpu.roll(upper, 2, 0)).astype(BF)
    odd_x = jnp.where(keep, pltpu.roll(lower, half - 2, 0), upper).astype(BF)
    rows = groups_y * 8
    for i in range(groups_x):
        out[(2 * i) * rows : (2 * i + 1) * rows] = even_x[i * rows : (i + 1) * rows]
        out[(2 * i + 1) * rows : (2 * i + 2) * rows] = odd_x[i * rows : (i + 1) * rows]

    for d in range(8):

        @pl.when(exists(d))
        def _():
            copy_of(d, False).wait_send()


def local(
    volume,
    first_weight,
    first_bias,
    second_weight,
    second_bias,
    inner_weight,
    inner_bias,
    outer_weight,
    outer_bias,
):
    size_x, size_y, size_z, chans = volume.shape
    gx, gy = size_x // 8, size_y // 8
    cells = gx * gy * 16
    any_spec = pl.BlockSpec(memory_space=pl.ANY)
    vmem = pltpu.VMEM
    result = pl.pallas_call(
        kernel,
        out_shape=jax.ShapeDtypeStruct((cells, 256), BF),
        in_specs=[any_spec] * 9,
        out_specs=pl.BlockSpec(memory_space=pltpu.VMEM),
        scratch_shapes=[
            vmem((gx, 8, size_y, size_z, chans), BF),
            vmem(first_weight.shape, BF),
            vmem(second_weight.shape, BF),
            vmem(inner_weight.shape, BF),
            vmem(outer_weight.shape, BF),
            vmem((1, 128), F32),
            vmem((1, 256), F32),
            vmem((1, 256), F32),
            vmem((1, 256), F32),
            vmem((gx * 8, 2, gy * 32, 128), F32),
            vmem((cells, 1024), BF),
            vmem((2, gx + 4, gy + 4, 8, 256), F32),
            vmem((2, gx + 2, gy + 2, 8, 256), F32),
            vmem((4, gy * 32, 256), BF),
            vmem((4, gy * 32, 256), BF),
            vmem((4, 64, 256), BF),
            vmem((4, 64, 256), BF),
            pltpu.SemaphoreType.DMA((gx + 12,)),
            pltpu.SemaphoreType.DMA((8,)),
            pltpu.SemaphoreType.DMA((8,)),
        ],
        compiler_params=pltpu.CompilerParams(
            collective_id=0, has_side_effects=True, vmem_limit_bytes=56 * 2**20
        ),
        cost_estimate=pl.CostEstimate(
            flops=2_000_000_000, bytes_accessed=12_000_000, transcendentals=0
        ),
    )(
        volume,
        first_weight,
        first_bias.reshape(1, -1),
        second_weight,
        second_bias.reshape(1, -1),
        inner_weight,
        inner_bias.reshape(1, -1),
        outer_weight,
        outer_bias.reshape(1, -1),
    )
    return result.reshape(size_x // 4, size_y // 4, size_z // 4, 256)


def solution(mesh):
    in_specs = (P("tx", "ty", None, None), P(), P(), P(), P(), P(), P(), P(), P())
    out_specs = P("tx", "ty", None, None)
    return jax.shard_map(local, mesh=mesh, in_specs=in_specs, out_specs=out_specs, check_vma=False)
```

```python
import jax
import jax.numpy as jnp
from jax import lax
from jax.experimental import pallas as pl
from jax.experimental.pallas import tpu as pltpu
from jax.sharding import PartitionSpec as P

MESSAGES = (
    (-1, 0, 0), (1, 0, 1),
    (-1, -1, 0), (-1, 1, 0), (0, -1, 0), (0, 1, 0),
    (1, -1, 1), (1, 1, 1), (0, -1, 1), (0, 1, 1),
)
PARTNER = (1, 0, 7, 6, 5, 4, 3, 2, 9, 8)
FIRST = (2, 3, 4, 5, 0)
SECOND = (6, 7, 8, 9, 1)
NEIGHBOURS = (0, 1, 2, 3, 4, 5, 6, 7)
BF = jnp.bfloat16
F32 = jnp.float32


def leaky(values):
    return jnp.where(values > 0, values, 0.01 * values)


def kernel(
    volume, w1, b1, w2, b2, wi, bi, wo, bo,
    out,
    vbuf, w1b, w2b, wib, wob, b1b, b2b, bib, bob,
    sums, blocks, halo, inner, edge_out, edge_in, corner_out, corner_in,
    load_sem, send_sem, recv_sem,
):
    ix, iy = lax.axis_index("tx"), lax.axis_index("ty")
    nx, ny = lax.axis_size("tx"), lax.axis_size("ty")
    groups_x, groups_y = halo.shape[1] - 4, halo.shape[2] - 4
    half = groups_x * groups_y * 8

    def exists(d):
        dx, dy, _ = MESSAGES[d]
        test = None
        for delta, i, n in ((dx, ix, nx), (dy, iy, ny)):
            if delta:
                one = i >= 1 if delta < 0 else i <= n - 2
                test = one if test is None else jnp.logical_and(test, one)
        return test

    def device(d):
        return {"tx": ix + MESSAGES[d][0], "ty": iy + MESSAGES[d][1]}

    loads = []

    def load(src, dst):
        copy = pltpu.make_async_copy(src, dst, load_sem.at[len(loads)])
        copy.start()
        loads.append(copy)
        return copy

    load_w1, load_b1 = load(w1, w1b), load(b1, b1b)
    load_v = [load(volume.at[pl.ds(8 * i, 8)], vbuf.at[i]) for i in range(groups_x)]
    load_w2, load_b2 = load(w2, w2b), load(b2, b2b)
    load_bi, load_bo = load(bi, bib), load(bo, bob)
    load_wi = {a: load(wi.at[a], wib.at[a]) for a in (1, 0, 2)}
    load_wo = {a: load(wo.at[a], wob.at[a]) for a in (1, 0, 2)}

    barrier = pltpu.get_barrier_semaphore()
    count = 0
    for d in NEIGHBOURS:
        count = count + exists(d).astype(jnp.int32)

        @pl.when(exists(d))
        def _():
            pl.semaphore_signal(
                barrier, inc=1, device_id=device(d), device_id_type=pl.DeviceIdType.MESH
            )

    halo[...] = jnp.zeros_like(halo)

    load_w1.wait()
    load_b1.wait()
    w1cat = jnp.concatenate(
        [
            jnp.concatenate([w1b[p, q, 0], w1b[p, q, 1]], axis=1)
            for p in range(2)
            for q in range(2)
        ],
        axis=0,
    )
    rows_y = 2 * groups_y
    bias1 = b1b[...]
    def first(i):
        load_v[i].wait()
        for xp in range(2):
            slabs = [
                vbuf[i, 4 * xp + j].reshape(rows_y, 4, 16, 64) for j in range(4)
            ]
            for pc in range(2):
                for qc in range(2):
                    lhs = jnp.concatenate(
                        [
                            slabs[2 * pc + p][:, 2 * qc + q].reshape(rows_y * 16, 64)
                            for p in range(2)
                            for q in range(2)
                        ],
                        axis=1,
                    )
                    slot = (i * 2 + xp) * 4 + pc * 2 + qc
                    both = jnp.dot(lhs, w1cat, preferred_element_type=F32)
                    sums[slot, 0] = both[:, 0:128]
                    sums[slot, 1] = both[:, 128:256]
            for pc in range(2):
                for qc in range(2):
                    slot = (i * 2 + xp) * 4 + pc * 2 + qc
                    for rc in range(2):
                        even = sums[slot, 0, pl.ds(2 * rc, 4 * rows_y, stride=4)]
                        odd = sums[slot, 1, pl.ds(2 * rc + 1, 4 * rows_y, stride=4)]
                        finer = leaky(even + odd + bias1).astype(BF)
                        k = (pc * 2 + qc) * 2 + rc
                        row = (i * 2 + xp) * 4 * rows_y
                        blocks[row : row + 4 * rows_y, k * 128 : k * 128 + 128] = finer

    def copy_of(d, incoming):
        slot = d if incoming else PARTNER[d]
        if d < 2:
            src, dst = edge_out.at[d], edge_in.at[slot]
        else:
            src, dst = corner_out.at[d - 2], corner_in.at[slot - 2]
        return pltpu.make_async_remote_copy(
            src_ref=src,
            dst_ref=dst,
            send_sem=send_sem.at[d],
            recv_sem=recv_sem.at[slot],
            device_id=device(d),
            device_id_type=pl.DeviceIdType.MESH,
        )

    def landed(d):
        dx, dy, h = MESSAGES[d]
        if dx:
            px = slice(0, 2) if dx < 0 else slice(groups_x + 2, groups_x + 4)
        else:
            px = slice(2 + 2 * h, 4 + 2 * h)
        if dy:
            return px, slice(0, 2) if dy < 0 else slice(groups_y + 2, groups_y + 4)
        return px, slice(2, 2 + groups_y)

    def second(h):
        rows = half
        total = jnp.dot(
            blocks[h * rows : h * rows + rows],
            w2b[...].reshape(8 * 128, 256),
            preferred_element_type=F32,
        )
        coarse = leaky(total + b2b[...]).astype(BF).astype(F32)
        coarse = coarse.reshape(groups_x // 2, 2, groups_y * 8, 256)
        rows = half // 2
        even_x = coarse[:, 0].reshape(rows, 256)
        odd_x = coarse[:, 1].reshape(rows, 256)
        keep = (lax.broadcasted_iota(jnp.int32, (rows, 256), 0) // 2) % 2 == 0
        parts = [
            part.reshape(groups_x // 2, groups_y, 8, 256)
            for part in (
                jnp.where(keep, even_x, pltpu.roll(odd_x, 2, 0)),
                jnp.where(keep, pltpu.roll(even_x, rows - 2, 0), odd_x),
            )
        ]
        for d in SECOND if h else FIRST:
            dy = MESSAGES[d][1]
            sy = slice(0, 2) if dy < 0 else slice(groups_y - 2, groups_y) if dy else slice(0, groups_y)
            block = jnp.concatenate([p[:, sy].reshape(-1, 256) for p in parts], axis=0).astype(BF)
            if d < 2:
                edge_out[d] = block
            else:
                corner_out[d - 2] = block

            @pl.when(exists(d))
            def _():
                copy_of(d, False).start()

        for z in range(2):
            halo[z, 2 + 2 * h : 4 + 2 * h, 2 : 2 + groups_y] = parts[z]

    per_half = groups_x // 2
    for i in range(per_half):
        first(i)
    load_w2.wait()
    load_b2.wait()
    pl.semaphore_wait(barrier, count)
    second(0)
    for i in range(per_half, groups_x):
        first(i)
    second(1)

    own = jnp.concatenate(
        [
            halo[z, 2 : 2 + groups_x, 2 : 2 + groups_y].reshape(half, 256).astype(BF)
            for z in range(2)
        ],
        axis=1,
    )
    keep = (lax.broadcasted_iota(jnp.int32, (half, 256), 0) // 2) % 2 == 0
    load_bi.wait()
    load_bo.wait()
    inner[...] = jnp.broadcast_to(bib[...].reshape(1, 1, 1, 1, 256), inner.shape)

    def both(lhs, weight, a, b):
        lower = weight[a, b, 1:3].reshape(512, 256)
        upper = weight[a, b, 0:2].reshape(512, 256)
        return (
            jnp.dot(lhs, lower, preferred_element_type=F32),
            jnp.dot(lhs, upper, preferred_element_type=F32),
        )

    for a in (1, 0, 2):
        load_wi[a].wait()
        for b in (1, 0, 2):
            for z, term in enumerate(both(own, wib, a, b)):
                inner[z, 2 - a : 2 - a + groups_x, 2 - b : 2 - b + groups_y] += term.reshape(
                    groups_x, groups_y, 8, 256
                )

    for d in FIRST + SECOND:
        px, py = landed(d)

        @pl.when(exists(d))
        def _():
            copy_of(d, True).wait_recv()
            block = (edge_in[d] if d < 2 else corner_in[d - 2]).astype(F32)
            rows = block.shape[0] // 2
            for z in range(2):
                shape = (px.stop - px.start, py.stop - py.start, 8, 256)
                halo[z, px, py] = block[z * rows : z * rows + rows].reshape(shape)

    def outside(shift, groups):
        return [i for i in range(shift, shift + groups + 2) if not 2 <= i < 2 + groups]

    for a in (1, 0, 2):
        for b in (1, 0, 2):
            pieces = [
                (slice(i, i + 1), slice(b, b + groups_y + 2)) for i in outside(a, groups_x)
            ] + [
                (slice(2, 2 + groups_x), slice(i, i + 1)) for i in outside(b, groups_y)
            ]
            lhs = jnp.concatenate(
                [
                    jnp.concatenate(
                        [halo[z, sx, sy].reshape(-1, 256) for sx, sy in pieces], axis=0
                    ).astype(BF)
                    for z in range(2)
                ],
                axis=1,
            )
            for z, term in enumerate(both(lhs, wib, a, b)):
                row = 0
                for sx, sy in pieces:
                    shape = (sx.stop - sx.start, sy.stop - sy.start, 8, 256)
                    rows = shape[0] * shape[1] * 8
                    inner[
                        z, sx.start - a : sx.stop - a, sy.start - b : sy.stop - b
                    ] += term[row : row + rows].reshape(shape)
                    row += rows

    inner[...] = leaky(inner[...]).astype(BF).astype(F32)

    @pl.when(ix == 0)
    def _():
        inner[:, 0] = jnp.zeros_like(inner[:, 0])

    @pl.when(ix == nx - 1)
    def _():
        inner[:, groups_x + 1] = jnp.zeros_like(inner[:, 0])

    @pl.when(iy == 0)
    def _():
        inner[:, :, 0] = jnp.zeros_like(inner[:, :, 0])

    @pl.when(iy == ny - 1)
    def _():
        inner[:, :, groups_y + 1] = jnp.zeros_like(inner[:, :, 0])

    totals = [
        halo[z, 2 : 2 + groups_x, 2 : 2 + groups_y].reshape(half, 256) + bob[...]
        for z in range(2)
    ]
    for a in (1, 0, 2):
        load_wo[a].wait()
        for b in (1, 0, 2):
            lhs = jnp.concatenate(
                [
                    inner[z, a : a + groups_x, b : b + groups_y].reshape(half, 256).astype(BF)
                    for z in range(2)
                ],
                axis=1,
            )
            totals = [t + term for t, term in zip(totals, both(lhs, wob, a, b))]
    lower, upper = leaky(totals[0]), leaky(totals[1])
    even_x = jnp.where(keep, lower, pltpu.roll(upper, 2, 0)).astype(BF)
    odd_x = jnp.where(keep, pltpu.roll(lower, half - 2, 0), upper).astype(BF)
    rows = groups_y * 8
    for i in range(groups_x):
        out[(2 * i) * rows : (2 * i + 1) * rows] = even_x[i * rows : (i + 1) * rows]
        out[(2 * i + 1) * rows : (2 * i + 2) * rows] = odd_x[i * rows : (i + 1) * rows]

    for d in range(10):

        @pl.when(exists(d))
        def _():
            copy_of(d, False).wait_send()


def local(
    volume,
    first_weight,
    first_bias,
    second_weight,
    second_bias,
    inner_weight,
    inner_bias,
    outer_weight,
    outer_bias,
):
    size_x, size_y, size_z, chans = volume.shape
    gx, gy = size_x // 8, size_y // 8
    cells = gx * gy * 16
    any_spec = pl.BlockSpec(memory_space=pl.ANY)
    vmem = pltpu.VMEM
    result = pl.pallas_call(
        kernel,
        out_shape=jax.ShapeDtypeStruct((cells, 256), BF),
        in_specs=[any_spec] * 9,
        out_specs=pl.BlockSpec(memory_space=pltpu.VMEM),
        scratch_shapes=[
            vmem((gx, 8, size_y, size_z, chans), BF),
            vmem(first_weight.shape, BF),
            vmem(second_weight.shape, BF),
            vmem(inner_weight.shape, BF),
            vmem(outer_weight.shape, BF),
            vmem((1, 128), F32),
            vmem((1, 256), F32),
            vmem((1, 256), F32),
            vmem((1, 256), F32),
            vmem((gx * 8, 2, gy * 32, 128), F32),
            vmem((cells, 1024), BF),
            vmem((2, gx + 4, gy + 4, 8, 256), F32),
            vmem((2, gx + 2, gy + 2, 8, 256), F32),
            vmem((2, gy * 32, 256), BF),
            vmem((2, gy * 32, 256), BF),
            vmem((8, 64, 256), BF),
            vmem((8, 64, 256), BF),
            pltpu.SemaphoreType.DMA((gx + 12,)),
            pltpu.SemaphoreType.DMA((10,)),
            pltpu.SemaphoreType.DMA((10,)),
        ],
        compiler_params=pltpu.CompilerParams(
            collective_id=0, has_side_effects=True, vmem_limit_bytes=56 * 2**20
        ),
        cost_estimate=pl.CostEstimate(
            flops=2_000_000_000, bytes_accessed=12_000_000, transcendentals=0
        ),
    )(
        volume,
        first_weight,
        first_bias.reshape(1, -1),
        second_weight,
        second_bias.reshape(1, -1),
        inner_weight,
        inner_bias.reshape(1, -1),
        outer_weight,
        outer_bias.reshape(1, -1),
    )
    return result.reshape(size_x // 4, size_y // 4, size_z // 4, 256)


def solution(mesh):
    in_specs = (P("tx", "ty", None, None), P(), P(), P(), P(), P(), P(), P(), P())
    out_specs = P("tx", "ty", None, None)
    return jax.shard_map(local, mesh=mesh, in_specs=in_specs, out_specs=out_specs, check_vma=False)
```
